32 devices in a mesh: au: 8 (over z, y), ia: 4 (over x, core).
Axes of the slice: x: 2, y: 2, z: 4, core: 2. Of those that a mesh axis runs over, the one named last changes fastest.
Arguments:
- user_emb: bfloat16 [8, 2048, 256], P('au', 'ia'), may hold values from -6 to 6
- item_emb: bfloat16 [4, 1024, 256], P('ia', 'au'), may hold values from -6 to 6
- weight: bfloat16 [256, 256], replicated, may hold values from -0.375 to 0.375
- grad_user: bfloat16 [8, 2048, 256], P('au', 'ia'), may hold values from -6 to 6
- grad_item: bfloat16 [4, 1024, 256], P('ia', 'au'), may hold values from -6 to 6
- tile_values: bfloat16 [8, 512, 128, 128], P('au', 'ia'), may hold values from 0 to 1
- tile_rows: int32 [8, 512], P('au', 'ia'), may hold values from 0 to 15
- tile_cols: int32 [8, 512], P('au', 'ia'), may hold values from 0 to 7
- tile_norm: int32 [8, 512], P('au', 'ia'), may hold values from 32 to 128
- tile_count: int32 [8, 4], P('au', 'ia'), may hold values from 64 to 128, as said below
Outputs:
- grad_user_emb: bfloat16 [8, 2048, 256], P('au', 'ia')
- grad_item_emb: bfloat16 [4, 1024, 256], P('ia', 'au')
- grad_weight: float32 [256, 256], replicated
The draws below stay inside these ranges and needn't reach their ends.
Inputs may be any that keep to these rules, and one draw needn't show every extreme that they name: `tile_rows`: slots of one block pair may name the same tile position; their terms add. Slots at and after tile_count[a, b] are unused; some block pair has exactly 128 live slots in every draw.
All inputs are finite; a program needn't handle non-finite values.
Results may differ from the reference program's by a relative error of at most 0.025.
Values may be sent and summed in bfloat16 or wider, within the bound.
A program may use at most 64 MiB of HBM per device.

```python
import math
import jax
import jax.numpy as jnp
from jax import lax

D = 256
TILE = 128
UT = 16
IT = 8
CAP = 128
USERS = 16384
ITEMS = 4096
N_AU = 8
N_IA = 4


def draw_tile_count(key, part):
    low_key, pick_key = jax.random.split(jax.random.fold_in(key, 7))
    counts = jax.random.randint(low_key, (N_AU * N_IA,), CAP // 2, CAP + 1)
    chosen = jax.random.randint(pick_key, (), 0, N_AU * N_IA)
    flattened = jnp.where(jnp.arange(N_AU * N_IA) == chosen, CAP, counts)
    return flattened.reshape(N_AU, N_IA).astype(jnp.int32)


def set_ends(values, stream_key, least, largest):
    longest = values.shape.index(max(values.shape))
    spots = []
    for shift in (0, 1):
        where = [jax.random.randint(jax.random.fold_in(stream_key, axis), (), 0, length) for axis, length in enumerate(values.shape)]
        where[longest] = (where[longest] + shift) % values.shape[longest]
        spots.append(tuple(where))
    return values.at[spots[0]].set(least).at[spots[1]].set(largest)


def level_of(stream_key, dims, pieces, least, top_value):
    level = 1.0
    for position, blocks in pieces:
        heights = jax.random.uniform(jax.random.fold_in(jax.random.fold_in(stream_key, 6), position), (blocks,), jnp.float32, least / len(pieces), top_value / len(pieces))
        level = level * jnp.repeat(jnp.exp(heights), dims[position] // blocks).reshape((-1,) + (1,) * (len(dims) - 1 - position))
    return level


def bell_draw(rng, extent, width, reach, cuts=(), kind=jnp.bfloat16):
    level = level_of(rng, extent, cuts, -0.22, 0.18) if cuts else 1.0
    values = jax.random.normal(rng, extent, jnp.float32) * width * level
    return jnp.minimum(jnp.maximum(values, -reach), reach).astype(kind)


def setup_inputs(seed: int = 0) -> dict:
    key_of = jax.random.split(jax.random.key(seed), 11)
    user_emb = bell_draw(key_of[0], (N_AU, UT * TILE, D), 1.0, 6.0, ((0, 8), (1, 4)))
    item_emb = bell_draw(key_of[1], (N_IA, IT * TILE, D), 1.0, 6.0, ((0, 4), (1, 8)))
    weight = bell_draw(key_of[2], (D, D), D ** -0.5, 0.375)
    grad_user = bell_draw(key_of[3], (N_AU, UT * TILE, D), 1.0, 6.0, ((0, 8), (1, 4)))
    grad_item = bell_draw(key_of[4], (N_IA, IT * TILE, D), 1.0, 6.0, ((0, 4), (1, 8)))
    tile_values = jnp.clip(1.0 * jax.random.uniform(key_of[5], (N_AU, N_IA * CAP, TILE, TILE), jnp.float32) ** level_of(key_of[5], (N_AU, N_IA * CAP, TILE, TILE), ((0, 8), (1, 4)), -0.2, 0.2), 0.0, 1.0).astype(jnp.bfloat16)
    tile_rows = set_ends(jax.random.randint(key_of[6], (N_AU, N_IA * CAP), 0, UT), jax.random.fold_in(key_of[6], 1), 0, UT - 1).astype(jnp.int32)
    tile_cols = set_ends(jax.random.randint(key_of[7], (N_AU, N_IA * CAP), 0, IT), jax.random.fold_in(key_of[7], 1), 0, IT - 1).astype(jnp.int32)
    tile_norm = set_ends(jax.random.randint(key_of[8], (N_AU, N_IA * CAP), 32, 129), jax.random.fold_in(key_of[8], 1), 32, 128).astype(jnp.int32)
    tile_count = draw_tile_count(jax.random.fold_in(key_of[10], 71), 0)
    return {"user_emb": user_emb, "item_emb": item_emb, "weight": weight, "grad_user": grad_user, "grad_item": grad_item, "tile_values": tile_values, "tile_rows": tile_rows, "tile_cols": tile_cols, "tile_norm": tile_norm, "tile_count": tile_count}


slot_group = 8

def rounded(value):
    return lax.optimization_barrier(value.astype(jnp.bfloat16)).astype(jnp.float32)

def device_terms(tile_block, row_ids, col_ids, norm_ids, live_count, item_source, user_source):
    turn_count = (live_count + slot_group - 1) // slot_group

    def one_turn(turn_index, totals):
        user_total, item_total = totals
        first_slot = (turn_index * slot_group).astype(jnp.int32)
        values = lax.dynamic_slice_in_dim(tile_block, first_slot, slot_group, 0).astype(jnp.float32)
        row_pick = lax.dynamic_slice_in_dim(row_ids, first_slot, slot_group, 0)
        col_pick = lax.dynamic_slice_in_dim(col_ids, first_slot, slot_group, 0)
        norm_pick = lax.dynamic_slice_in_dim(norm_ids, first_slot, slot_group, 0)
        live_mask = first_slot + jnp.arange(slot_group, dtype=jnp.int32) < live_count
        inverse = jnp.where(live_mask, 1.0 / norm_pick.astype(jnp.float32), 0.0)[:, None, None]
        forward = jnp.einsum('gic,gcd->gid', values, item_source[col_pick].astype(jnp.float32))
        user_total = user_total.at[row_pick].add(forward * inverse)
        backward = jnp.einsum('gic,gid->gcd', values, user_source[row_pick].astype(jnp.float32))
        item_total = item_total.at[col_pick].add(backward * inverse)
        return (user_total, item_total)
    start = (jnp.zeros(user_source.shape, jnp.float32), jnp.zeros(item_source.shape, jnp.float32))
    return lax.fori_loop(jnp.int32(0), turn_count.astype(jnp.int32), one_turn, start)

def reference(user_emb, item_emb, weight, grad_user, grad_item, tile_values, tile_rows, tile_cols, tile_norm, tile_count):

    def per_user_block(item_sum, block_index):
        user_source = grad_user[block_index].reshape(UT, TILE, D)
        block_values = tile_values[block_index]
        block_rows = tile_rows[block_index]
        block_cols = tile_cols[block_index]
        block_norms = tile_norm[block_index]

        def per_item_block(carry, item_index):
            user_total, item_sum = carry
            item_source = grad_item[item_index].reshape(IT, TILE, D)
            slot_start = (item_index * CAP).astype(jnp.int32)
            part_user, part_item = device_terms(lax.dynamic_slice_in_dim(block_values, slot_start, CAP, 0), lax.dynamic_slice_in_dim(block_rows, slot_start, CAP, 0), lax.dynamic_slice_in_dim(block_cols, slot_start, CAP, 0), lax.dynamic_slice_in_dim(block_norms, slot_start, CAP, 0), tile_count[block_index, item_index], item_source, user_source)
            current = lax.dynamic_index_in_dim(item_sum, item_index, 0, keepdims=False)
            item_sum = lax.dynamic_update_index_in_dim(item_sum, current + rounded(part_item).reshape(IT * TILE, D), item_index, 0)
            return ((user_total + rounded(part_user), item_sum), None)
        start = (jnp.zeros((UT, TILE, D), jnp.float32), item_sum)
        (user_total, item_sum), unused = lax.scan(per_item_block, start, jnp.arange(N_IA, dtype=jnp.int32))
        return (item_sum, user_total.reshape(UT * TILE, D))
    q_item, q_user = lax.scan(per_user_block, jnp.zeros((N_IA, IT * TILE, D), jnp.float32), jnp.arange(N_AU, dtype=jnp.int32))
    q_user_low = rounded(q_user)
    q_item_low = rounded(q_item)
    weight_wide = weight.astype(jnp.float32)
    grad_user_emb = jnp.einsum('bre,de->brd', q_user_low, weight_wide).astype(jnp.bfloat16)
    grad_item_emb = jnp.einsum('bre,de->brd', q_item_low, weight_wide).astype(jnp.bfloat16)
    user_term = jnp.einsum('brd,bre->de', user_emb.astype(jnp.float32), q_user, precision=lax.Precision.HIGHEST)
    item_term = jnp.einsum('brd,bre->de', item_emb.astype(jnp.float32), q_item, precision=lax.Precision.HIGHEST)
    grad_weight = (user_term + item_term) / math.sqrt(USERS + ITEMS)
    return (grad_user_emb, grad_item_emb, grad_weight)
```

```python
import functools
import math

import jax
import jax.numpy as jnp
from jax import lax
from jax.experimental import pallas as pl
from jax.experimental.pallas import tpu as pltpu
from jax.sharding import PartitionSpec as P

MESH = pl.DeviceIdType.MESH
LOAD_PARTS = 8
LANES = 128


def remote(src, dst, send_sem, recv_sem, target):
    return pltpu.make_async_remote_copy(
        src_ref=src,
        dst_ref=dst,
        send_sem=send_sem,
        recv_sem=recv_sem,
        device_id=target,
        device_id_type=MESH,
    )


def block_of(ref, index, rows):
    return ref.at[pl.ds(pl.multiple_of(index * rows, rows), rows)]


def take(ref, index, rows):
    return ref[pl.ds(pl.multiple_of(index * rows, rows), rows), :]


class Ring:
    def __init__(self, axis, size):
        self.axis = axis
        self.half = size // 2
        self.me = lax.axis_index(axis)
        self.pair = self.me // 2
        self.side = self.me % 2

    def ahead(self, step):
        return (self.pair + step) % self.half

    def behind(self, step):
        return (self.pair + self.half - step) % self.half

    def same(self, pair):
        return 2 * pair + self.side

    def other(self, pair):
        return 2 * pair + 1 - self.side

    def at(self, index):
        return {self.axis: index}


class Gather:
    def __init__(self, ring, shard, full, sems):
        self.ring, self.shard, self.full = ring, shard, full
        self.rows = shard.shape[0]
        self.near_send, self.near_recv, self.far_send, self.far_recv = sems

    def near(self, step, arriving=False):
        ring = self.ring
        target = ring.other(ring.pair) if step == 0 else ring.same(ring.ahead(step))
        origin = ring.other(ring.pair) if step == 0 else ring.same(ring.behind(step))
        block = block_of(self.full, origin if arriving else ring.me, self.rows)
        return remote(
            self.shard, block, self.near_send.at[step], self.near_recv.at[step], ring.at(target)
        )

    def far(self, step, arriving=False):
        ring = self.ring
        behind = ring.behind(step)
        source = block_of(self.full, ring.same(behind), self.rows)
        landing = block_of(self.full, ring.other(behind), self.rows) if arriving else source
        return remote(
            source,
            landing,
            self.far_send.at[step],
            self.far_recv.at[step],
            ring.at(ring.other(ring.pair)),
        )

    def start(self):
        for step in range(1, self.ring.half):
            self.near(step).start()
        self.near(0).start()

    def keep_own(self):
        self.full[pl.ds(pl.multiple_of(self.ring.me * self.rows, self.rows), self.rows), :] = (
            self.shard[...]
        )

    def forward(self, step):
        self.near(step, True).wait_recv()
        self.far(step).start()

    def finish(self):
        self.near(0, True).wait_recv()
        for step in range(1, self.ring.half):
            self.far(step, True).wait_recv()

    def drain(self):
        for step in range(self.ring.half):
            self.near(step).wait_send()
        for step in range(1, self.ring.half):
            self.far(step).wait_send()


class Reduce:
    def __init__(self, ring, terms, near_land, far_out, far_land, sems):
        self.ring, self.terms = ring, terms
        self.near_land, self.far_out, self.far_land = near_land, far_out, far_land
        self.rows = near_land.shape[1]
        self.near_send, self.near_recv, self.far_send, self.far_recv = sems

    def near(self, step):
        ring = self.ring
        return remote(
            block_of(self.terms, ring.other(ring.ahead(step)), self.rows),
            self.near_land.at[step],
            self.near_send.at[step],
            self.near_recv.at[step],
            ring.at(ring.other(ring.pair)),
        )

    def far(self, step):
        ring = self.ring
        return remote(
            self.far_out.at[step],
            self.far_land.at[step],
            self.far_send.at[step],
            self.far_recv.at[step],
            ring.at(ring.same(ring.ahead(step))),
        )

    def order(self):
        return [*range(1, self.ring.half), 0]

    def start(self):
        for step in self.order():
            self.near(step).start()

    def joined(self, step):
        self.near(step).wait_recv()
        mine = take(self.terms, self.ring.same(self.ring.ahead(step)), self.rows)
        return mine.astype(jnp.float32) + self.near_land[step].astype(jnp.float32)

    def pass_on(self):
        for step in range(1, self.ring.half):
            self.far_out[step] = self.joined(step).astype(jnp.bfloat16)
            self.far(step).start()

    def finish(self):
        total = self.joined(0)
        for step in range(1, self.ring.half):
            self.far(step).wait_recv()
            total = total + self.far_land[step].astype(jnp.float32)
        return total

    def drain(self):
        for step in range(self.ring.half):
            self.near(step).wait_send()
        for step in range(1, self.ring.half):
            self.far(step).wait_send()


def dot(left, right, dims):
    return lax.dot_general(left, right, (dims, ((), ())), preferred_element_type=jnp.float32)


def embedded_product(embedded, total, low):
    rest = (total - low.astype(jnp.float32)).astype(jnp.bfloat16)
    return dot(embedded, low, ((0,), (0,))) + dot(embedded, rest, ((0,), (0,)))


def kernel(
    sizes,
    link_ref,
    scale_ref,
    user_emb,
    item_emb,
    weight,
    grad_user,
    grad_item,
    tiles_hbm,
    out_user,
    out_item,
    out_weight,
    tiles,
    sums,
    adjacency,
    user_full,
    item_full,
    user_terms,
    item_terms,
    user_near,
    user_out,
    user_far,
    item_near,
    item_out,
    item_far,
    piece_out,
    piece_land,
    piece_own,
    piece_all,
    load_sem,
    ia_gather_sems,
    au_gather_sems,
    ia_reduce_sems,
    au_reduce_sems,
    piece_sems,
):
    n_au, n_ia, in_kernel, factor = sizes
    count = n_au * n_ia
    cap, edge = tiles.shape[0], tiles.shape[1]
    users, items = adjacency.shape
    user_tiles, item_tiles = users // edge, items // edge
    au, ia = Ring("au", n_au), Ring("ia", n_ia)
    me = au.me * n_ia + ia.me

    def peer(index):
        return (index // n_ia, index % n_ia)

    part = cap // LOAD_PARTS

    def load(index):
        span = pl.ds(index * part, part)
        return pltpu.make_async_copy(tiles_hbm.at[span], tiles.at[span], load_sem.at[index])

    for index in range(LOAD_PARTS):
        load(index).start()

    barrier = pltpu.get_barrier_semaphore()
    if in_kernel:

        def greet(step, carry):
            pl.semaphore_signal(
                barrier, inc=1, device_id=peer((me + step) % count), device_id_type=MESH
            )
            return carry

        lax.fori_loop(1, count, greet, 0)
        pl.semaphore_wait(barrier, count - 1)
    else:
        for ring in (au, ia):
            pl.semaphore_signal(
                barrier, inc=1, device_id=ring.at(ring.other(ring.pair)), device_id_type=MESH
            )
            for step in range(1, ring.half):
                pl.semaphore_signal(
                    barrier,
                    inc=1,
                    device_id=ring.at(ring.same(ring.ahead(step))),
                    device_id_type=MESH,
                )
        pl.semaphore_wait(barrier, au.half + ia.half)

    gather_user = Gather(ia, grad_user, user_full, [ia_gather_sems.at[i] for i in range(4)])
    gather_item = Gather(au, grad_item, item_full, [au_gather_sems.at[i] for i in range(4)])
    gather_item.start()
    gather_user.start()
    gather_user.keep_own()
    gather_item.keep_own()

    sums[0] = jnp.zeros(sums.shape[1:], jnp.float32)

    def add_slot(slot, carry):
        sums[slot + 1] = (
            tiles[slot].astype(jnp.float32) * scale_ref[slot] + sums[link_ref[slot]]
        )
        return carry

    for index in range(LOAD_PARTS):
        load(index).wait()
        lax.fori_loop(index * part, (index + 1) * part, add_slot, 0)

    for step in range(1, min(au.half, 2)):
        gather_item.forward(step)

    def place_row(row, carry):
        for column in range(item_tiles):
            tile = sums[link_ref[cap + row * item_tiles + column]]
            adjacency[
                pl.ds(pl.multiple_of(row * edge, edge), edge), pl.ds(column * edge, edge)
            ] = tile.astype(jnp.bfloat16)
        return carry

    lax.fori_loop(0, user_tiles, place_row, 0)

    for step in range(2, au.half):
        gather_item.forward(step)
    for step in range(1, ia.half):
        gather_user.forward(step)

    wide = 2 * edge
    gather_user.finish()

    def item_product(index, carry):
        start = pl.multiple_of(index * wide, wide)
        product = dot(adjacency[:, pl.ds(start, wide)], user_full[...], ((0,), (0,)))
        item_terms[pl.ds(start, wide), :] = product.astype(jnp.bfloat16)
        return carry

    lax.fori_loop(0, items // wide, item_product, 0)
    reduce_item = Reduce(
        au, item_terms, item_near, item_out, item_far, [au_reduce_sems.at[i] for i in range(4)]
    )
    reduce_item.start()

    gather_item.finish()

    def user_product(index, carry):
        start = pl.multiple_of(index * wide, wide)
        product = dot(adjacency[pl.ds(start, wide), :], item_full[...], ((1,), (0,)))
        user_terms[pl.ds(start, wide), :] = product.astype(jnp.bfloat16)
        return carry

    lax.fori_loop(0, users // wide, user_product, 0)
    reduce_user = Reduce(
        ia, user_terms, user_near, user_out, user_far, [ia_reduce_sems.at[i] for i in range(4)]
    )
    reduce_user.start()
    reduce_user.pass_on()
    reduce_item.pass_on()

    q_user = reduce_user.finish()
    user_low = q_user.astype(jnp.bfloat16)
    out_user[...] = dot(user_low, weight[...], ((1,), (1,))).astype(jnp.bfloat16)
    term = embedded_product(user_emb[...], q_user, user_low)
    q_item = reduce_item.finish()
    item_low = q_item.astype(jnp.bfloat16)
    term = term + embedded_product(item_emb[...], q_item, item_low)

    if in_kernel:
        piece_rows = piece_out.shape[1]
        columns = out_weight.shape[1] // LANES
        for index in range(count):
            row, column = index // columns, index % columns
            piece_out[index] = term[
                row * piece_rows : (row + 1) * piece_rows, column * LANES : (column + 1) * LANES
            ].astype(jnp.bfloat16)

        def scatter(step):
            target = (me + step) % count
            return remote(
                piece_out.at[target],
                piece_land.at[step],
                piece_sems.at[0, step],
                piece_sems.at[1, step],
                peer(target),
            )

        def spread(step, arriving=False):
            origin = (me + count - step) % count
            return remote(
                piece_own,
                piece_all.at[origin if arriving else me],
                piece_sems.at[2, step],
                piece_sems.at[3, step],
                peer((me + step) % count),
            )

        def run(action):
            def body(step, carry):
                action(step)
                return carry

            lax.fori_loop(1, count, body, 0)

        run(lambda step: scatter(step).start())
        out_item[...] = dot(item_low, weight[...], ((1,), (1,))).astype(jnp.bfloat16)
        run(lambda step: scatter(step).wait_recv())
        total = piece_out[me].astype(jnp.float32)
        for step in range(1, count):
            total = total + piece_land[step].astype(jnp.float32)
        piece_own[...] = total.astype(jnp.bfloat16)
        run(lambda step: spread(step).start())
        piece_all[me] = piece_own[...]
        run(lambda step: spread(step, True).wait_recv())
        for index in range(count):
            row, column = index // columns, index % columns
            out_weight[
                row * piece_rows : (row + 1) * piece_rows, column * LANES : (column + 1) * LANES
            ] = (piece_all[index].astype(jnp.float32) * factor)
        run(lambda step: scatter(step).wait_send())
        run(lambda step: spread(step).wait_send())
    else:
        out_item[...] = dot(item_low, weight[...], ((1,), (1,))).astype(jnp.bfloat16)
        out_weight[...] = term * factor

    gather_user.drain()
    gather_item.drain()
    reduce_user.drain()
    reduce_item.drain()


def per_device(
    user_emb,
    item_emb,
    weight,
    grad_user,
    grad_item,
    tile_values,
    tile_rows,
    tile_cols,
    tile_norm,
    tile_count,
):
    n_au, n_ia = lax.axis_size("au"), lax.axis_size("ia")
    count = n_au * n_ia
    width = weight.shape[0]
    cap, edge = tile_values.shape[1:3]
    user_rows, item_rows = user_emb.shape[1], item_emb.shape[1]
    users, items = user_rows * n_ia, item_rows * n_au
    item_tiles = items // edge
    places = (users // edge) * item_tiles

    slots = jnp.arange(cap, dtype=jnp.int32)
    live = slots < tile_count[0, 0]
    place = jnp.where(live, tile_rows[0] * item_tiles + tile_cols[0], -1)
    wanted = jnp.concatenate([place, jnp.arange(places, dtype=jnp.int32)])
    limit = jnp.concatenate([slots, jnp.full((places,), cap, jnp.int32)])
    match = (place[None] == wanted[:, None]) & (slots[None] < limit[:, None])
    links = jnp.max(jnp.where(match, slots[None] + 1, 0), axis=1)
    scale = jnp.where(live, 1.0 / tile_norm[0].astype(jnp.float32), 0.0)

    piece_rows = width * (width // LANES) // count
    in_kernel = piece_rows % 16 == 0 and piece_rows > 0 and width % piece_rows == 0
    pieces = count if in_kernel else 1
    piece_rows = piece_rows if in_kernel else 16
    factor = 1.0 / math.sqrt(users * n_au + items * n_ia)
    half_au, half_ia = n_au // 2, n_ia // 2
    bf16, f32 = jnp.bfloat16, jnp.float32
    vmem = pl.BlockSpec(memory_space=pltpu.VMEM)
    smem = pl.BlockSpec(memory_space=pltpu.SMEM)
    dma = pltpu.SemaphoreType.DMA

    outs = pl.pallas_call(
        functools.partial(kernel, (n_au, n_ia, in_kernel, factor)),
        out_shape=(
            jax.ShapeDtypeStruct((user_rows, width), bf16),
            jax.ShapeDtypeStruct((item_rows, width), bf16),
            jax.ShapeDtypeStruct((width, width), f32),
        ),
        in_specs=[smem, smem, vmem, vmem, vmem, vmem, vmem, pl.BlockSpec(memory_space=pl.ANY)],
        out_specs=(vmem, vmem, vmem),
        scratch_shapes=[
            pltpu.VMEM((cap, edge, edge), bf16),
            pltpu.VMEM((cap + 1, edge, edge), f32),
            pltpu.VMEM((users, items), bf16),
            pltpu.VMEM((users, width), bf16),
            pltpu.VMEM((items, width), bf16),
            pltpu.VMEM((users, width), bf16),
            pltpu.VMEM((items, width), bf16),
            pltpu.VMEM((half_ia, user_rows, width), bf16),
            pltpu.VMEM((half_ia, user_rows, width), bf16),
            pltpu.VMEM((half_ia, user_rows, width), bf16),
            pltpu.VMEM((half_au, item_rows, width), bf16),
            pltpu.VMEM((half_au, item_rows, width), bf16),
            pltpu.VMEM((half_au, item_rows, width), bf16),
            pltpu.VMEM((pieces, piece_rows, LANES), bf16),
            pltpu.VMEM((pieces, piece_rows, LANES), bf16),
            pltpu.VMEM((piece_rows, LANES), bf16),
            pltpu.VMEM((pieces, piece_rows, LANES), bf16),
            dma((LOAD_PARTS,)),
            dma((4, half_ia)),
            dma((4, half_au)),
            dma((4, half_ia)),
            dma((4, half_au)),
            dma((4, pieces)),
        ],
        compiler_params=pltpu.CompilerParams(
            collective_id=0, has_side_effects=True, vmem_limit_bytes=44 * 1024 * 1024
        ),
    )(
        links,
        scale,
        user_emb[0],
        item_emb[0],
        weight,
        grad_user[0],
        grad_item[0],
        tile_values[0],
    )
    grad_user_emb, grad_item_emb, grad_weight = outs
    if not in_kernel:
        grad_weight = lax.psum(grad_weight, ("au", "ia"))
    return (grad_user_emb[None], grad_item_emb[None], grad_weight)


def solution(mesh):
    return jax.shard_map(
        per_device,
        mesh=mesh,
        in_specs=(
            P("au", "ia", None),
            P("ia", "au", None),
            P(),
            P("au", "ia", None),
            P("ia", "au", None),
            P("au", "ia", None, None),
            P("au", "ia"),
            P("au", "ia"),
            P("au", "ia"),
            P("au", "ia"),
        ),
        out_specs=(P("au", "ia", None), P("ia", "au", None), P()),
        check_vma=False,
    )
```

```python
import functools
import math

import jax
import jax.numpy as jnp
from jax import lax
from jax.experimental import pallas as pl
from jax.experimental.pallas import tpu as pltpu
from jax.sharding import PartitionSpec as P

MESH = pl.DeviceIdType.MESH
LOAD_PARTS = 8
LANES = 128


def remote(src, dst, send_sem, recv_sem, target):
    return pltpu.make_async_remote_copy(
        src_ref=src,
        dst_ref=dst,
        send_sem=send_sem,
        recv_sem=recv_sem,
        device_id=target,
        device_id_type=MESH,
    )


def block_of(ref, index, rows):
    return ref.at[pl.ds(pl.multiple_of(index * rows, rows), rows)]


def take(ref, index, rows):
    return ref[pl.ds(pl.multiple_of(index * rows, rows), rows), :]


class Ring:
    def __init__(self, axis, size):
        self.axis = axis
        self.half = size // 2
        self.me = lax.axis_index(axis)
        self.pair = self.me // 2
        self.side = self.me % 2

    def ahead(self, step):
        return (self.pair + step) % self.half

    def behind(self, step):
        return (self.pair + self.half - step) % self.half

    def same(self, pair):
        return 2 * pair + self.side

    def other(self, pair):
        return 2 * pair + 1 - self.side

    def at(self, index):
        return {self.axis: index}


class Gather:
    def __init__(self, ring, shard, full, sems):
        self.ring, self.shard, self.full = ring, shard, full
        self.rows = shard.shape[0]
        self.near_send, self.near_recv, self.far_send, self.far_recv = sems

    def near(self, step, arriving=False):
        ring = self.ring
        target = ring.other(ring.pair) if step == 0 else ring.same(ring.ahead(step))
        origin = ring.other(ring.pair) if step == 0 else ring.same(ring.behind(step))
        block = block_of(self.full, origin if arriving else ring.me, self.rows)
        return remote(
            self.shard, block, self.near_send.at[step], self.near_recv.at[step], ring.at(target)
        )

    def far(self, step, arriving=False):
        ring = self.ring
        behind = ring.behind(step)
        source = block_of(self.full, ring.same(behind), self.rows)
        landing = block_of(self.full, ring.other(behind), self.rows) if arriving else source
        return remote(
            source,
            landing,
            self.far_send.at[step],
            self.far_recv.at[step],
            ring.at(ring.other(ring.pair)),
        )

    def start(self):
        for step in range(1, self.ring.half):
            self.near(step).start()
        self.near(0).start()

    def forward(self, step):
        self.near(step, True).wait_recv()
        self.far(step).start()

    def finish(self):
        self.near(0, True).wait_recv()
        for step in range(1, self.ring.half):
            self.far(step, True).wait_recv()

    def drain(self):
        for step in range(self.ring.half):
            self.near(step).wait_send()
        for step in range(1, self.ring.half):
            self.far(step).wait_send()


class Reduce:
    def __init__(self, ring, terms, near_land, far_out, far_land, sems):
        self.ring, self.terms = ring, terms
        self.near_land, self.far_out, self.far_land = near_land, far_out, far_land
        self.rows = near_land.shape[1]
        self.near_send, self.near_recv, self.far_send, self.far_recv = sems

    def near(self, step):
        ring = self.ring
        return remote(
            block_of(self.terms, ring.other(ring.ahead(step)), self.rows),
            self.near_land.at[step],
            self.near_send.at[step],
            self.near_recv.at[step],
            ring.at(ring.other(ring.pair)),
        )

    def far(self, step):
        ring = self.ring
        return remote(
            self.far_out.at[step],
            self.far_land.at[step],
            self.far_send.at[step],
            self.far_recv.at[step],
            ring.at(ring.same(ring.ahead(step))),
        )

    def order(self):
        return [*range(1, self.ring.half), 0]

    def start(self):
        for step in self.order():
            self.near(step).start()

    def joined(self, step):
        self.near(step).wait_recv()
        mine = take(self.terms, self.ring.same(self.ring.ahead(step)), self.rows)
        return mine.astype(jnp.float32) + self.near_land[step].astype(jnp.float32)

    def pass_on(self):
        for step in range(1, self.ring.half):
            self.far_out[step] = self.joined(step).astype(jnp.bfloat16)
            self.far(step).start()

    def finish(self):
        total = self.joined(0)
        for step in range(1, self.ring.half):
            self.far(step).wait_recv()
            total = total + self.far_land[step].astype(jnp.float32)
        return total

    def drain(self):
        for step in range(self.ring.half):
            self.near(step).wait_send()
        for step in range(1, self.ring.half):
            self.far(step).wait_send()


def dot(left, right, dims):
    return lax.dot_general(left, right, (dims, ((), ())), preferred_element_type=jnp.float32)


def embedded_product(embedded, total, low):
    rest = (total - low.astype(jnp.float32)).astype(jnp.bfloat16)
    return dot(embedded, low, ((0,), (0,))) + dot(embedded, rest, ((0,), (0,)))


def slot_links(rows, columns, live_count, item_tiles, places):
    cap = rows.shape[1]
    lane = lax.broadcasted_iota(jnp.int32, (cap, cap), 1)
    slot = lax.broadcasted_iota(jnp.int32, (cap, cap), 0)
    place = jnp.broadcast_to(rows * item_tiles + columns, (cap, cap))
    place = jnp.where(lane < live_count, place, -1)
    held = place.T
    earlier = jnp.where((held == place) & (slot < lane) & (held >= 0), slot + 1, 0)
    links = [jnp.max(earlier, axis=0, keepdims=True)]
    for first in range(0, places, cap):
        latest = jnp.where(held == lane + first, slot + 1, 0)
        links.append(jnp.max(latest, axis=0, keepdims=True))
    return links


def kernel(
    sizes,
    count_ref,
    tile_rows,
    tile_cols,
    tile_norm,
    user_emb_hbm,
    item_emb_hbm,
    weight_hbm,
    grad_user,
    grad_item,
    tiles_hbm,
    out_user,
    out_item,
    out_weight,
    user_emb,
    item_emb,
    weight,
    tables,
    link_rows,
    scale_row,
    link_ref,
    scale_ref,
    tiles,
    sums,
    adjacency,
    user_full,
    item_full,
    user_terms,
    item_terms,
    user_near,
    user_out,
    user_far,
    item_near,
    item_out,
    item_far,
    piece_out,
    piece_land,
    piece_own,
    piece_all,
    load_sem,
    own_sem,
    table_sem,
    ia_gather_sems,
    au_gather_sems,
    ia_reduce_sems,
    au_reduce_sems,
    piece_sems,
):
    n_au, n_ia, in_kernel, factor = sizes
    count = n_au * n_ia
    cap, edge = tiles.shape[0], tiles.shape[1]
    users, items = adjacency.shape
    user_tiles, item_tiles = users // edge, items // edge
    au, ia = Ring("au", n_au), Ring("ia", n_ia)
    me = au.me * n_ia + ia.me

    def peer(index):
        return (index // n_ia, index % n_ia)

    part = cap // LOAD_PARTS

    def load(index):
        span = pl.ds(index * part, part)
        return pltpu.make_async_copy(tiles_hbm.at[span], tiles.at[span], load_sem.at[index])

    table_loads = [
        pltpu.make_async_copy(source, tables.at[index], table_sem.at[index])
        for index, source in enumerate((tile_rows, tile_cols, tile_norm))
    ]
    for copy in table_loads:
        copy.start()
    for index in range(LOAD_PARTS):
        load(index).start()

    def own(full, shard, ring, index):
        rows = shard.shape[0]
        return pltpu.make_async_copy(shard, block_of(full, ring.me, rows), own_sem.at[index])

    own_loads = [
        own(user_full, grad_user, ia, 0),
        own(item_full, grad_item, au, 1),
        pltpu.make_async_copy(user_emb_hbm, user_emb, own_sem.at[2]),
        pltpu.make_async_copy(item_emb_hbm, item_emb, own_sem.at[3]),
        pltpu.make_async_copy(weight_hbm, weight, own_sem.at[4]),
    ]
    for copy in own_loads:
        copy.start()

    barrier = pltpu.get_barrier_semaphore()
    if in_kernel:

        def greet(step, carry):
            pl.semaphore_signal(
                barrier, inc=1, device_id=peer((me + step) % count), device_id_type=MESH
            )
            return carry

        lax.fori_loop(1, count, greet, 0)
        pl.semaphore_wait(barrier, count - 1)
    else:
        for ring in (au, ia):
            pl.semaphore_signal(
                barrier, inc=1, device_id=ring.at(ring.other(ring.pair)), device_id_type=MESH
            )
            for step in range(1, ring.half):
                pl.semaphore_signal(
                    barrier,
                    inc=1,
                    device_id=ring.at(ring.same(ring.ahead(step))),
                    device_id_type=MESH,
                )
        pl.semaphore_wait(barrier, au.half + ia.half)

    gather_user = Gather(ia, grad_user, user_full, [ia_gather_sems.at[i] for i in range(4)])
    gather_item = Gather(au, grad_item, item_full, [au_gather_sems.at[i] for i in range(4)])
    gather_item.start()
    gather_user.start()

    for copy in table_loads:
        copy.wait()
    places = user_tiles * item_tiles
    live_count = count_ref[0, 0]
    links = slot_links(tables[0], tables[1], live_count, item_tiles, places)
    for index, row in enumerate(links):
        link_rows[index : index + 1, :] = row
    alive = lax.broadcasted_iota(jnp.int32, (1, cap), 1) < live_count
    scale_row[...] = jnp.where(alive, 1.0 / tables[2].astype(jnp.float32), 0.0)
    to_scalars = [
        pltpu.make_async_copy(link_rows, link_ref, table_sem.at[3]),
        pltpu.make_async_copy(scale_row, scale_ref, table_sem.at[4]),
    ]
    for copy in to_scalars:
        copy.start()
    for copy in to_scalars:
        copy.wait()

    sums[0] = jnp.zeros(sums.shape[1:], jnp.float32)

    def add_slot(slot, carry):
        sums[slot + 1] = (
            tiles[slot].astype(jnp.float32) * scale_ref[0, slot] + sums[link_ref[0, slot]]
        )
        return carry

    for index in range(LOAD_PARTS):
        load(index).wait()
        lax.fori_loop(index * part, (index + 1) * part, add_slot, 0)

    for step in range(1, min(au.half, 2)):
        gather_item.forward(step)

    def place_row(row, carry):
        for column in range(item_tiles):
            place = row * item_tiles + column
            tile = sums[link_ref[1 + place // cap, place % cap]]
            adjacency[
                pl.ds(pl.multiple_of(row * edge, edge), edge), pl.ds(column * edge, edge)
            ] = tile.astype(jnp.bfloat16)
        return carry

    lax.fori_loop(0, user_tiles, place_row, 0)

    for step in range(2, au.half):
        gather_item.forward(step)
    for step in range(1, ia.half):
        gather_user.forward(step)

    wide = 2 * edge
    for copy in own_loads:
        copy.wait()
    gather_user.finish()

    def item_product(index, carry):
        start = pl.multiple_of(index * wide, wide)
        product = dot(adjacency[:, pl.ds(start, wide)], user_full[...], ((0,), (0,)))
        item_terms[pl.ds(start, wide), :] = product.astype(jnp.bfloat16)
        return carry

    lax.fori_loop(0, items // wide, item_product, 0)
    reduce_item = Reduce(
        au, item_terms, item_near, item_out, item_far, [au_reduce_sems.at[i] for i in range(4)]
    )
    reduce_item.start()

    gather_item.finish()

    def user_product(index, carry):
        start = pl.multiple_of(index * wide, wide)
        product = dot(adjacency[pl.ds(start, wide), :], item_full[...], ((1,), (0,)))
        user_terms[pl.ds(start, wide), :] = product.astype(jnp.bfloat16)
        return carry

    lax.fori_loop(0, users // wide, user_product, 0)
    reduce_user = Reduce(
        ia, user_terms, user_near, user_out, user_far, [ia_reduce_sems.at[i] for i in range(4)]
    )
    reduce_user.start()
    reduce_user.pass_on()
    reduce_item.pass_on()

    q_user = reduce_user.finish()
    user_low = q_user.astype(jnp.bfloat16)
    out_user[...] = dot(user_low, weight[...], ((1,), (1,))).astype(jnp.bfloat16)
    term = embedded_product(user_emb[...], q_user, user_low)
    q_item = reduce_item.finish()
    item_low = q_item.astype(jnp.bfloat16)
    term = term + embedded_product(item_emb[...], q_item, item_low)

    if in_kernel:
        piece_rows = piece_out.shape[1]
        columns = out_weight.shape[1] // LANES
        for index in range(count):
            row, column = index // columns, index % columns
            piece_out[index] = term[
                row * piece_rows : (row + 1) * piece_rows, column * LANES : (column + 1) * LANES
            ].astype(jnp.bfloat16)

        def scatter(step):
            target = (me + step) % count
            return remote(
                piece_out.at[target],
                piece_land.at[step],
                piece_sems.at[0, step],
                piece_sems.at[1, step],
                peer(target),
            )

        def spread(step, arriving=False):
            origin = (me + count - step) % count
            return remote(
                piece_own,
                piece_all.at[origin if arriving else me],
                piece_sems.at[2, step],
                piece_sems.at[3, step],
                peer((me + step) % count),
            )

        def run(action):
            for step in range(1, count):
                action(step)

        run(lambda step: scatter(step).start())
        out_item[...] = dot(item_low, weight[...], ((1,), (1,))).astype(jnp.bfloat16)
        run(lambda step: scatter(step).wait_recv())
        total = piece_out[me].astype(jnp.float32)
        for step in range(1, count):
            total = total + piece_land[step].astype(jnp.float32)
        piece_own[...] = total.astype(jnp.bfloat16)
        run(lambda step: spread(step).start())
        piece_all[me] = piece_own[...]
        run(lambda step: spread(step, True).wait_recv())
        for index in range(count):
            row, column = index // columns, index % columns
            out_weight[
                row * piece_rows : (row + 1) * piece_rows, column * LANES : (column + 1) * LANES
            ] = (piece_all[index].astype(jnp.float32) * factor)
        run(lambda step: scatter(step).wait_send())
        run(lambda step: spread(step).wait_send())
    else:
        out_item[...] = dot(item_low, weight[...], ((1,), (1,))).astype(jnp.bfloat16)
        out_weight[...] = term * factor

    gather_user.drain()
    gather_item.drain()
    reduce_user.drain()
    reduce_item.drain()


def per_device(
    user_emb,
    item_emb,
    weight,
    grad_user,
    grad_item,
    tile_values,
    tile_rows,
    tile_cols,
    tile_norm,
    tile_count,
):
    n_au, n_ia = lax.axis_size("au"), lax.axis_size("ia")
    count = n_au * n_ia
    width = weight.shape[0]
    cap, edge = tile_values.shape[1:3]
    user_rows, item_rows = user_emb.shape[1], item_emb.shape[1]
    users, items = user_rows * n_ia, item_rows * n_au
    item_tiles = items // edge
    places = (users // edge) * item_tiles

    link_rows = 1 + -(-places // cap)
    piece_rows = width * (width // LANES) // count
    in_kernel = piece_rows % 16 == 0 and piece_rows > 0 and width % piece_rows == 0
    pieces = count if in_kernel else 1
    piece_rows = piece_rows if in_kernel else 16
    factor = 1.0 / math.sqrt(users * n_au + items * n_ia)
    half_au, half_ia = n_au // 2, n_ia // 2
    bf16, f32 = jnp.bfloat16, jnp.float32
    vmem = pl.BlockSpec(memory_space=pltpu.VMEM)
    smem = pl.BlockSpec(memory_space=pltpu.SMEM)
    dma = pltpu.SemaphoreType.DMA

    outs = pl.pallas_call(
        functools.partial(kernel, (n_au, n_ia, in_kernel, factor)),
        out_shape=(
            jax.ShapeDtypeStruct((user_rows, width), bf16),
            jax.ShapeDtypeStruct((item_rows, width), bf16),
            jax.ShapeDtypeStruct((width, width), f32),
        ),
        in_specs=[smem] + [pl.BlockSpec(memory_space=pltpu.HBM)] * 9,
        out_specs=(vmem, vmem, vmem),
        scratch_shapes=[
            pltpu.VMEM((user_rows, width), bf16),
            pltpu.VMEM((item_rows, width), bf16),
            pltpu.VMEM((width, width), bf16),
            pltpu.VMEM((3, 1, cap), jnp.int32),
            pltpu.VMEM((link_rows, cap), jnp.int32),
            pltpu.VMEM((1, cap), f32),
            pltpu.SMEM((link_rows, cap), jnp.int32),
            pltpu.SMEM((1, cap), f32),
            pltpu.VMEM((cap, edge, edge), bf16),
            pltpu.VMEM((cap + 1, edge, edge), f32),
            pltpu.VMEM((users, items), bf16),
            pltpu.VMEM((users, width), bf16),
            pltpu.VMEM((items, width), bf16),
            pltpu.VMEM((users, width), bf16),
            pltpu.VMEM((items, width), bf16),
            pltpu.VMEM((half_ia, user_rows, width), bf16),
            pltpu.VMEM((half_ia, user_rows, width), bf16),
            pltpu.VMEM((half_ia, user_rows, width), bf16),
            pltpu.VMEM((half_au, item_rows, width), bf16),
            pltpu.VMEM((half_au, item_rows, width), bf16),
            pltpu.VMEM((half_au, item_rows, width), bf16),
            pltpu.VMEM((pieces, piece_rows, LANES), bf16),
            pltpu.VMEM((pieces, piece_rows, LANES), bf16),
            pltpu.VMEM((piece_rows, LANES), bf16),
            pltpu.VMEM((pieces, piece_rows, LANES), bf16),
            dma((LOAD_PARTS,)),
            dma((5,)),
            dma((5,)),
            dma((4, half_ia)),
            dma((4, half_au)),
            dma((4, half_ia)),
            dma((4, half_au)),
            dma((4, pieces)),
        ],
        compiler_params=pltpu.CompilerParams(
            collective_id=0, has_side_effects=True, vmem_limit_bytes=62 * 1024 * 1024
        ),
    )(
        tile_count,
        tile_rows,
        tile_cols,
        tile_norm,
        user_emb[0],
        item_emb[0],
        weight,
        grad_user[0],
        grad_item[0],
        tile_values[0],
    )
    grad_user_emb, grad_item_emb, grad_weight = outs
    if not in_kernel:
        grad_weight = lax.psum(grad_weight, ("au", "ia"))
    return (grad_user_emb[None], grad_item_emb[None], grad_weight)


def solution(mesh):
    return jax.shard_map(
        per_device,
        mesh=mesh,
        in_specs=(
            P("au", "ia", None),
            P("ia", "au", None),
            P(),
            P("au", "ia", None),
            P("ia", "au", None),
            P("au", "ia", None, None),
            P("au", "ia"),
            P("au", "ia"),
            P("au", "ia"),
            P("au", "ia"),
        ),
        out_specs=(P("au", "ia", None), P("ia", "au", None), P()),
        check_vma=False,
    )
```

```python
import functools
import math

import jax
import jax.numpy as jnp
from jax import lax
from jax.experimental import pallas as pl
from jax.experimental.pallas import tpu as pltpu
from jax.sharding import PartitionSpec as P

MESH = pl.DeviceIdType.MESH
LOAD_PARTS = 8
LANES = 128


def remote(src, dst, send_sem, recv_sem, target):
    return pltpu.make_async_remote_copy(
        src_ref=src,
        dst_ref=dst,
        send_sem=send_sem,
        recv_sem=recv_sem,
        device_id=target,
        device_id_type=MESH,
    )


def block_of(ref, index, rows):
    return ref.at[pl.ds(pl.multiple_of(index * rows, rows), rows)]


def take(ref, index, rows):
    return ref[pl.ds(pl.multiple_of(index * rows, rows), rows), :]


class Ring:
    def __init__(self, axis, size):
        self.axis = axis
        self.half = size // 2
        self.me = lax.axis_index(axis)
        self.pair = self.me // 2
        self.side = self.me % 2

    def ahead(self, step):
        return (self.pair + step) % self.half

    def behind(self, step):
        return (self.pair + self.half - step) % self.half

    def same(self, pair):
        return 2 * pair + self.side

    def other(self, pair):
        return 2 * pair + 1 - self.side

    def at(self, index):
        return {self.axis: index}


class Gather:
    def __init__(self, ring, shard, full, sems):
        self.ring, self.shard, self.full = ring, shard, full
        self.rows = shard.shape[0]
        self.near_send, self.near_recv, self.far_send, self.far_recv = sems

    def near(self, step, arriving=False):
        ring = self.ring
        target = ring.other(ring.pair) if step == 0 else ring.same(ring.ahead(step))
        origin = ring.other(ring.pair) if step == 0 else ring.same(ring.behind(step))
        block = block_of(self.full, origin if arriving else ring.me, self.rows)
        return remote(
            self.shard, block, self.near_send.at[step], self.near_recv.at[step], ring.at(target)
        )

    def far(self, step, arriving=False):
        ring = self.ring
        behind = ring.behind(step)
        source = block_of(self.full, ring.same(behind), self.rows)
        landing = block_of(self.full, ring.other(behind), self.rows) if arriving else source
        return remote(
            source,
            landing,
            self.far_send.at[step],
            self.far_recv.at[step],
            ring.at(ring.other(ring.pair)),
        )

    def start(self):
        for step in range(1, self.ring.half):
            self.near(step).start()
        self.near(0).start()

    def forward(self, step):
        self.near(step, True).wait_recv()
        self.far(step).start()

    def finish(self):
        self.near(0, True).wait_recv()
        for step in range(1, self.ring.half):
            self.far(step, True).wait_recv()

    def drain(self):
        for step in range(self.ring.half):
            self.near(step).wait_send()
        for step in range(1, self.ring.half):
            self.far(step).wait_send()


class Reduce:
    def __init__(self, ring, terms, near_land, far_out, far_land, sems):
        self.ring, self.terms = ring, terms
        self.near_land, self.far_out, self.far_land = near_land, far_out, far_land
        self.rows = near_land.shape[1]
        self.near_send, self.near_recv, self.far_send, self.far_recv = sems

    def near(self, step):
        ring = self.ring
        return remote(
            block_of(self.terms, ring.other(ring.ahead(step)), self.rows),
            self.near_land.at[step],
            self.near_send.at[step],
            self.near_recv.at[step],
            ring.at(ring.other(ring.pair)),
        )

    def far(self, step):
        ring = self.ring
        return remote(
            self.far_out.at[step],
            self.far_land.at[step],
            self.far_send.at[step],
            self.far_recv.at[step],
            ring.at(ring.same(ring.ahead(step))),
        )

    def order(self):
        return [*range(1, self.ring.half), 0]

    def start(self):
        for step in self.order():
            self.near(step).start()

    def joined(self, step):
        self.near(step).wait_recv()
        mine = take(self.terms, self.ring.same(self.ring.ahead(step)), self.rows)
        return mine.astype(jnp.float32) + self.near_land[step].astype(jnp.float32)

    def pass_on(self):
        for step in range(1, self.ring.half):
            self.far_out[step] = self.joined(step).astype(jnp.bfloat16)
            self.far(step).start()

    def finish(self):
        total = self.joined(0)
        for step in range(1, self.ring.half):
            self.far(step).wait_recv()
            total = total + self.far_land[step].astype(jnp.float32)
        return total

    def drain(self):
        for step in range(self.ring.half):
            self.near(step).wait_send()
        for step in range(1, self.ring.half):
            self.far(step).wait_send()


def dot(left, right, dims):
    return lax.dot_general(left, right, (dims, ((), ())), preferred_element_type=jnp.float32)


def embedded_product(embedded, total, low):
    rest = (total - low.astype(jnp.float32)).astype(jnp.bfloat16)
    return dot(embedded, low, ((0,), (0,))) + dot(embedded, rest, ((0,), (0,)))


def slot_links(rows, columns, live_count, item_tiles, places):
    cap = rows.shape[1]
    lane = lax.broadcasted_iota(jnp.int32, (cap, cap), 1)
    slot = lax.broadcasted_iota(jnp.int32, (cap, cap), 0)
    place = jnp.broadcast_to(rows * item_tiles + columns, (cap, cap))
    place = jnp.where(lane < live_count, place, -1)
    held = place.T
    earlier = jnp.where((held == place) & (slot < lane) & (held >= 0), slot + 1, 0)
    links = [jnp.max(earlier, axis=0, keepdims=True)]
    for first in range(0, places, cap):
        latest = jnp.where(held == lane + first, slot + 1, 0)
        links.append(jnp.max(latest, axis=0, keepdims=True))
    return links


def kernel(
    sizes,
    count_ref,
    tile_rows,
    tile_cols,
    tile_norm,
    user_emb_hbm,
    item_emb_hbm,
    weight_hbm,
    grad_user,
    grad_item,
    tiles_hbm,
    out_user_hbm,
    out_item_hbm,
    out_weight,
    out_user,
    out_item,
    user_emb,
    item_emb,
    weight,
    tables,
    link_rows,
    scale_row,
    link_ref,
    scale_ref,
    tiles,
    sums,
    adjacency,
    user_full,
    item_full,
    user_terms,
    item_terms,
    user_near,
    user_out,
    user_far,
    item_near,
    item_out,
    item_far,
    piece_out,
    piece_land,
    piece_own,
    piece_all,
    load_sem,
    own_sem,
    table_sem,
    ia_gather_sems,
    au_gather_sems,
    ia_reduce_sems,
    au_reduce_sems,
    piece_sems,
):
    n_au, n_ia, in_kernel, factor = sizes
    count = n_au * n_ia
    cap, edge = tiles.shape[0], tiles.shape[1]
    users, items = adjacency.shape
    user_tiles, item_tiles = users // edge, items // edge
    au, ia = Ring("au", n_au), Ring("ia", n_ia)
    me = au.me * n_ia + ia.me

    def peer(index):
        return (index // n_ia, index % n_ia)

    part = cap // LOAD_PARTS

    def load(index):
        span = pl.ds(index * part, part)
        return pltpu.make_async_copy(tiles_hbm.at[span], tiles.at[span], load_sem.at[index])

    table_loads = [
        pltpu.make_async_copy(source, tables.at[index], table_sem.at[index])
        for index, source in enumerate((tile_rows, tile_cols, tile_norm))
    ]
    for copy in table_loads:
        copy.start()
    for index in range(LOAD_PARTS):
        load(index).start()

    def own(full, shard, ring, index):
        rows = shard.shape[0]
        return pltpu.make_async_copy(shard, block_of(full, ring.me, rows), own_sem.at[index])

    own_loads = [
        own(user_full, grad_user, ia, 0),
        own(item_full, grad_item, au, 1),
        pltpu.make_async_copy(user_emb_hbm, user_emb, own_sem.at[2]),
        pltpu.make_async_copy(item_emb_hbm, item_emb, own_sem.at[3]),
        pltpu.make_async_copy(weight_hbm, weight, own_sem.at[4]),
    ]
    for copy in own_loads:
        copy.start()

    barrier = pltpu.get_barrier_semaphore()
    for ring in (au, ia):
        for step in range(ring.half):
            index = ring.same(ring.ahead(step)) if step else ring.other(ring.pair)
            pl.semaphore_signal(barrier, inc=1, device_id=ring.at(index), device_id_type=MESH)
    pl.semaphore_wait(barrier, au.half + ia.half)

    gather_user = Gather(ia, grad_user, user_full, [ia_gather_sems.at[i] for i in range(4)])
    gather_item = Gather(au, grad_item, item_full, [au_gather_sems.at[i] for i in range(4)])
    gather_item.start()
    gather_user.start()

    for copy in table_loads:
        copy.wait()
    places = user_tiles * item_tiles
    live_count = count_ref[0, 0]
    links = slot_links(tables[0], tables[1], live_count, item_tiles, places)
    for index, row in enumerate(links):
        link_rows[index : index + 1, :] = row
    alive = lax.broadcasted_iota(jnp.int32, (1, cap), 1) < live_count
    scale_row[...] = jnp.where(alive, 1.0 / tables[2].astype(jnp.float32), 0.0)
    to_scalars = [
        pltpu.make_async_copy(link_rows, link_ref, table_sem.at[3]),
        pltpu.make_async_copy(scale_row, scale_ref, table_sem.at[4]),
    ]
    for copy in to_scalars:
        copy.start()
    for copy in to_scalars:
        copy.wait()

    sums[0] = jnp.zeros(sums.shape[1:], jnp.float32)

    def add_slot(slot, carry):
        sums[slot + 1] = (
            tiles[slot].astype(jnp.float32) * scale_ref[0, slot] + sums[link_ref[0, slot]]
        )
        return carry

    for index in range(LOAD_PARTS):
        load(index).wait()
        lax.fori_loop(index * part, (index + 1) * part, add_slot, 0)

    for step in range(1, min(au.half, 2)):
        gather_item.forward(step)

    def place_row(row, carry):
        for column in range(item_tiles):
            place = row * item_tiles + column
            tile = sums[link_ref[1 + place // cap, place % cap]]
            adjacency[
                pl.ds(pl.multiple_of(row * edge, edge), edge), pl.ds(column * edge, edge)
            ] = tile.astype(jnp.bfloat16)
        return carry

    lax.fori_loop(0, user_tiles, place_row, 0)

    for step in range(2, au.half):
        gather_item.forward(step)
    for step in range(1, ia.half):
        gather_user.forward(step)

    wide = 2 * edge
    for copy in own_loads:
        copy.wait()
    gather_user.finish()

    def item_product(index, carry):
        start = pl.multiple_of(index * wide, wide)
        product = dot(adjacency[:, pl.ds(start, wide)], user_full[...], ((0,), (0,)))
        item_terms[pl.ds(start, wide), :] = product.astype(jnp.bfloat16)
        return carry

    lax.fori_loop(0, items // wide, item_product, 0)
    reduce_item = Reduce(
        au, item_terms, item_near, item_out, item_far, [au_reduce_sems.at[i] for i in range(4)]
    )
    reduce_item.start()

    gather_item.finish()

    def user_product(index, carry):
        start = pl.multiple_of(index * wide, wide)
        product = dot(adjacency[pl.ds(start, wide), :], item_full[...], ((1,), (0,)))
        user_terms[pl.ds(start, wide), :] = product.astype(jnp.bfloat16)
        return carry

    lax.fori_loop(0, users // wide, user_product, 0)
    reduce_user = Reduce(
        ia, user_terms, user_near, user_out, user_far, [ia_reduce_sems.at[i] for i in range(4)]
    )
    reduce_user.start()
    reduce_user.pass_on()
    reduce_item.pass_on()

    q_user = reduce_user.finish()
    user_low = q_user.astype(jnp.bfloat16)
    out_user[...] = dot(user_low, weight[...], ((1,), (1,))).astype(jnp.bfloat16)
    keep_user = pltpu.make_async_copy(out_user, out_user_hbm, own_sem.at[5])
    keep_item = pltpu.make_async_copy(out_item, out_item_hbm, own_sem.at[6])
    keep_user.start()
    term = embedded_product(user_emb[...], q_user, user_low)
    q_item = reduce_item.finish()
    item_low = q_item.astype(jnp.bfloat16)
    term = term + embedded_product(item_emb[...], q_item, item_low)

    if in_kernel:
        piece_rows = piece_out.shape[1]
        columns = out_weight.shape[1] // LANES
        for index in range(count):
            row, column = index // columns, index % columns
            piece_out[index] = term[
                row * piece_rows : (row + 1) * piece_rows, column * LANES : (column + 1) * LANES
            ].astype(jnp.bfloat16)

        def scatter(step):
            target = (me + step) % count
            return remote(
                piece_out.at[target],
                piece_land.at[step],
                piece_sems.at[0, step],
                piece_sems.at[1, step],
                peer(target),
            )

        def spread(step, arriving=False):
            origin = (me + count - step) % count
            return remote(
                piece_own,
                piece_all.at[origin if arriving else me],
                piece_sems.at[2, step],
                piece_sems.at[3, step],
                peer((me + step) % count),
            )

        def run(action):
            for step in range(1, count):
                action(step)

        run(lambda step: scatter(step).start())
        out_item[...] = dot(item_low, weight[...], ((1,), (1,))).astype(jnp.bfloat16)
        keep_item.start()
        run(lambda step: scatter(step).wait_recv())
        total = piece_out[me].astype(jnp.float32)
        for step in range(1, count):
            total = total + piece_land[step].astype(jnp.float32)
        piece_own[...] = total.astype(jnp.bfloat16)
        run(lambda step: spread(step).start())
        piece_all[me] = piece_own[...]
        run(lambda step: spread(step, True).wait_recv())
        for index in range(count):
            row, column = index // columns, index % columns
            out_weight[
                row * piece_rows : (row + 1) * piece_rows, column * LANES : (column + 1) * LANES
            ] = (piece_all[index].astype(jnp.float32) * factor)
        run(lambda step: scatter(step).wait_send())
        run(lambda step: spread(step).wait_send())
    else:
        out_item[...] = dot(item_low, weight[...], ((1,), (1,))).astype(jnp.bfloat16)
        keep_item.start()
        out_weight[...] = term * factor

    keep_user.wait()
    keep_item.wait()
    gather_user.drain()
    gather_item.drain()
    reduce_user.drain()
    reduce_item.drain()


def per_device(
    user_emb,
    item_emb,
    weight,
    grad_user,
    grad_item,
    tile_values,
    tile_rows,
    tile_cols,
    tile_norm,
    tile_count,
):
    n_au, n_ia = lax.axis_size("au"), lax.axis_size("ia")
    count = n_au * n_ia
    width = weight.shape[0]
    cap, edge = tile_values.shape[1:3]
    user_rows, item_rows = user_emb.shape[1], item_emb.shape[1]
    users, items = user_rows * n_ia, item_rows * n_au
    item_tiles = items // edge
    places = (users // edge) * item_tiles

    link_rows = 1 + -(-places // cap)
    piece_rows = width * (width // LANES) // count
    in_kernel = piece_rows % 16 == 0 and piece_rows > 0 and width % piece_rows == 0
    pieces = count if in_kernel else 1
    piece_rows = piece_rows if in_kernel else 16
    factor = 1.0 / math.sqrt(users * n_au + items * n_ia)
    half_au, half_ia = n_au // 2, n_ia // 2
    bf16, f32 = jnp.bfloat16, jnp.float32
    vmem = pl.BlockSpec(memory_space=pltpu.VMEM)
    hbm = pl.BlockSpec(memory_space=pltpu.HBM)
    smem = pl.BlockSpec(memory_space=pltpu.SMEM)
    dma = pltpu.SemaphoreType.DMA

    outs = pl.pallas_call(
        functools.partial(kernel, (n_au, n_ia, in_kernel, factor)),
        out_shape=(
            jax.ShapeDtypeStruct((user_rows, width), bf16),
            jax.ShapeDtypeStruct((item_rows, width), bf16),
            jax.ShapeDtypeStruct((width, width), f32),
        ),
        in_specs=[smem] + [hbm] * 9,
        out_specs=(hbm, hbm, vmem),
        scratch_shapes=[
            pltpu.VMEM((user_rows, width), bf16),
            pltpu.VMEM((item_rows, width), bf16),
            pltpu.VMEM((user_rows, width), bf16),
            pltpu.VMEM((item_rows, width), bf16),
            pltpu.VMEM((width, width), bf16),
            pltpu.VMEM((3, 1, cap), jnp.int32),
            pltpu.VMEM((link_rows, cap), jnp.int32),
            pltpu.VMEM((1, cap), f32),
            pltpu.SMEM((link_rows, cap), jnp.int32),
            pltpu.SMEM((1, cap), f32),
            pltpu.VMEM((cap, edge, edge), bf16),
            pltpu.VMEM((cap + 1, edge, edge), f32),
            pltpu.VMEM((users, items), bf16),
            pltpu.VMEM((users, width), bf16),
            pltpu.VMEM((items, width), bf16),
            pltpu.VMEM((users, width), bf16),
            pltpu.VMEM((items, width), bf16),
            pltpu.VMEM((half_ia, user_rows, width), bf16),
            pltpu.VMEM((half_ia, user_rows, width), bf16),
            pltpu.VMEM((half_ia, user_rows, width), bf16),
            pltpu.VMEM((half_au, item_rows, width), bf16),
            pltpu.VMEM((half_au, item_rows, width), bf16),
            pltpu.VMEM((half_au, item_rows, width), bf16),
            pltpu.VMEM((pieces, piece_rows, LANES), bf16),
            pltpu.VMEM((pieces, piece_rows, LANES), bf16),
            pltpu.VMEM((piece_rows, LANES), bf16),
            pltpu.VMEM((pieces, piece_rows, LANES), bf16),
            dma((LOAD_PARTS,)),
            dma((7,)),
            dma((5,)),
            dma((4, half_ia)),
            dma((4, half_au)),
            dma((4, half_ia)),
            dma((4, half_au)),
            dma((4, pieces)),
        ],
        compiler_params=pltpu.CompilerParams(
            collective_id=0, has_side_effects=True, vmem_limit_bytes=62 * 1024 * 1024
        ),
    )(
        tile_count,
        tile_rows,
        tile_cols,
        tile_norm,
        user_emb[0],
        item_emb[0],
        weight,
        grad_user[0],
        grad_item[0],
        tile_values[0],
    )
    grad_user_emb, grad_item_emb, grad_weight = outs
    if not in_kernel:
        grad_weight = lax.psum(grad_weight, ("au", "ia"))
    return (grad_user_emb[None], grad_item_emb[None], grad_weight)


def solution(mesh):
    return jax.shard_map(
        per_device,
        mesh=mesh,
        in_specs=(
            P("au", "ia", None),
            P("ia", "au", None),
            P(),
            P("au", "ia", None),
            P("ia", "au", None),
            P("au", "ia", None, None),
            P("au", "ia"),
            P("au", "ia"),
            P("au", "ia"),
            P("au", "ia"),
        ),
        out_specs=(P("au", "ia", None), P("ia", "au", None), P()),
        check_vma=False,
    )
```

```python
import functools
import math

import jax
import jax.numpy as jnp
from jax import lax
from jax.experimental import pallas as pl
from jax.experimental.pallas import tpu as pltpu
from jax.sharding import PartitionSpec as P

MESH = pl.DeviceIdType.MESH
LOAD_PARTS = 8
LANES = 128


def remote(src, dst, send_sem, recv_sem, target):
    return pltpu.make_async_remote_copy(
        src_ref=src,
        dst_ref=dst,
        send_sem=send_sem,
        recv_sem=recv_sem,
        device_id=target,
        device_id_type=MESH,
    )


def block_of(ref, index, rows):
    return ref.at[pl.ds(pl.multiple_of(index * rows, rows), rows)]


def take(ref, index, rows):
    return ref[pl.ds(pl.multiple_of(index * rows, rows), rows), :]


class Ring:
    def __init__(self, axis, size):
        self.axis = axis
        self.half = size // 2
        self.me = lax.axis_index(axis)
        self.pair = self.me // 2
        self.side = self.me % 2

    def ahead(self, step):
        return (self.pair + step) % self.half

    def behind(self, step):
        return (self.pair + self.half - step) % self.half

    def same(self, pair):
        return 2 * pair + self.side

    def other(self, pair):
        return 2 * pair + 1 - self.side

    def at(self, index):
        return {self.axis: index}


class Gather:
    def __init__(self, ring, shard, full, sems):
        self.ring, self.shard, self.full = ring, shard, full
        self.rows = shard.shape[0]
        self.near_send, self.near_recv, self.far_send, self.far_recv = sems

    def near(self, step, arriving=False):
        ring = self.ring
        target = ring.other(ring.pair) if step == 0 else ring.same(ring.ahead(step))
        origin = ring.other(ring.pair) if step == 0 else ring.same(ring.behind(step))
        block = block_of(self.full, origin if arriving else ring.me, self.rows)
        return remote(
            self.shard, block, self.near_send.at[step], self.near_recv.at[step], ring.at(target)
        )

    def far(self, step, arriving=False):
        ring = self.ring
        behind = ring.behind(step)
        source = block_of(self.full, ring.same(behind), self.rows)
        landing = block_of(self.full, ring.other(behind), self.rows) if arriving else source
        return remote(
            source,
            landing,
            self.far_send.at[step],
            self.far_recv.at[step],
            ring.at(ring.other(ring.pair)),
        )

    def start(self):
        for step in range(1, self.ring.half):
            self.near(step).start()
        self.near(0).start()

    def forward(self, step):
        self.near(step, True).wait_recv()
        self.far(step).start()

    def finish(self):
        self.near(0, True).wait_recv()
        for step in range(1, self.ring.half):
            self.far(step, True).wait_recv()

    def drain(self):
        for step in range(self.ring.half):
            self.near(step).wait_send()
        for step in range(1, self.ring.half):
            self.far(step).wait_send()


class Reduce:
    def __init__(self, ring, terms, near_land, far_out, far_land, sems):
        self.ring, self.terms = ring, terms
        self.near_land, self.far_out, self.far_land = near_land, far_out, far_land
        self.rows = near_land.shape[1]
        self.near_send, self.near_recv, self.far_send, self.far_recv = sems

    def near(self, step):
        ring = self.ring
        return remote(
            block_of(self.terms, ring.other(ring.ahead(step)), self.rows),
            self.near_land.at[step],
            self.near_send.at[step],
            self.near_recv.at[step],
            ring.at(ring.other(ring.pair)),
        )

    def far(self, step):
        ring = self.ring
        return remote(
            self.far_out.at[step],
            self.far_land.at[step],
            self.far_send.at[step],
            self.far_recv.at[step],
            ring.at(ring.same(ring.ahead(step))),
        )

    def order(self):
        return [*range(1, self.ring.half), 0]

    def start(self):
        for step in self.order():
            self.near(step).start()

    def joined(self, step):
        self.near(step).wait_recv()
        mine = take(self.terms, self.ring.same(self.ring.ahead(step)), self.rows)
        return mine.astype(jnp.float32) + self.near_land[step].astype(jnp.float32)

    def pass_on(self):
        for step in range(1, self.ring.half):
            self.far_out[step] = self.joined(step).astype(jnp.bfloat16)
            self.far(step).start()

    def finish(self):
        total = self.joined(0)
        for step in range(1, self.ring.half):
            self.far(step).wait_recv()
            total = total + self.far_land[step].astype(jnp.float32)
        return total

    def drain(self):
        for step in range(self.ring.half):
            self.near(step).wait_send()
        for step in range(1, self.ring.half):
            self.far(step).wait_send()


def dot(left, right, dims):
    return lax.dot_general(left, right, (dims, ((), ())), preferred_element_type=jnp.float32)


def embedded_product(embedded, total, low):
    rest = (total - low.astype(jnp.float32)).astype(jnp.bfloat16)
    return dot(embedded, low, ((0,), (0,))) + dot(embedded, rest, ((0,), (0,)))


def slot_links(rows, columns, live_count, item_tiles, places):
    cap = rows.shape[1]
    lane = lax.broadcasted_iota(jnp.int32, (cap, cap), 1)
    slot = lax.broadcasted_iota(jnp.int32, (cap, cap), 0)
    place = jnp.broadcast_to(rows * item_tiles + columns, (cap, cap))
    place = jnp.where(lane < live_count, place, -1)
    held = place.T
    earlier = jnp.where((held == place) & (slot < lane) & (held >= 0), slot + 1, 0)
    links = [jnp.max(earlier, axis=0, keepdims=True)]
    for first in range(0, places, cap):
        latest = jnp.where(held == lane + first, slot + 1, 0)
        links.append(jnp.max(latest, axis=0, keepdims=True))
    return links


def kernel(
    sizes,
    count_ref,
    tile_rows,
    tile_cols,
    tile_norm,
    user_emb_hbm,
    item_emb_hbm,
    weight_hbm,
    grad_user,
    grad_item,
    tiles_hbm,
    out_user_hbm,
    out_item_hbm,
    out_weight,
    out_user,
    out_item,
    user_emb,
    item_emb,
    weight,
    tables,
    link_rows,
    scale_row,
    link_ref,
    scale_ref,
    tiles,
    sums,
    adjacency,
    user_full,
    item_full,
    user_terms,
    item_terms,
    user_near,
    user_out,
    user_far,
    item_near,
    item_out,
    item_far,
    piece_out,
    piece_land,
    piece_own,
    piece_all,
    load_sem,
    own_sem,
    table_sem,
    ia_gather_sems,
    au_gather_sems,
    ia_reduce_sems,
    au_reduce_sems,
    piece_sems,
):
    n_au, n_ia, in_kernel, factor = sizes
    count = n_au * n_ia
    cap, edge = tiles.shape[0], tiles.shape[1]
    users, items = adjacency.shape
    user_tiles, item_tiles = users // edge, items // edge
    au, ia = Ring("au", n_au), Ring("ia", n_ia)
    me = au.me * n_ia + ia.me

    def peer(index):
        return (index // n_ia, index % n_ia)

    part = cap // LOAD_PARTS

    def load(index):
        span = pl.ds(index * part, part)
        return pltpu.make_async_copy(tiles_hbm.at[span], tiles.at[span], load_sem.at[index])

    table_loads = [
        pltpu.make_async_copy(source, tables.at[index], table_sem.at[index])
        for index, source in enumerate((tile_rows, tile_cols, tile_norm))
    ]
    for copy in table_loads:
        copy.start()
    for index in range(LOAD_PARTS):
        load(index).start()

    def own(full, shard, ring, index):
        rows = shard.shape[0]
        return pltpu.make_async_copy(shard, block_of(full, ring.me, rows), own_sem.at[index])

    own_loads = [
        own(user_full, grad_user, ia, 0),
        own(item_full, grad_item, au, 1),
        pltpu.make_async_copy(user_emb_hbm, user_emb, own_sem.at[2]),
        pltpu.make_async_copy(item_emb_hbm, item_emb, own_sem.at[3]),
        pltpu.make_async_copy(weight_hbm, weight, own_sem.at[4]),
    ]
    for copy in own_loads:
        copy.start()

    barrier = pltpu.get_barrier_semaphore()
    for ring in (au, ia):
        for step in range(ring.half):
            index = ring.same(ring.ahead(step)) if step else ring.other(ring.pair)
            pl.semaphore_signal(barrier, inc=1, device_id=ring.at(index), device_id_type=MESH)
    pl.semaphore_wait(barrier, au.half + ia.half)

    gather_user = Gather(ia, grad_user, user_full, [ia_gather_sems.at[i] for i in range(4)])
    gather_item = Gather(au, grad_item, item_full, [au_gather_sems.at[i] for i in range(4)])
    gather_item.start()
    gather_user.start()

    for copy in table_loads:
        copy.wait()
    places = user_tiles * item_tiles
    live_count = count_ref[0, 0]
    links = slot_links(tables[0], tables[1], live_count, item_tiles, places)
    for index, row in enumerate(links):
        link_rows[index : index + 1, :] = row
    alive = lax.broadcasted_iota(jnp.int32, (1, cap), 1) < live_count
    scale_row[...] = jnp.where(alive, 1.0 / tables[2].astype(jnp.float32), 0.0)
    to_scalars = [
        pltpu.make_async_copy(link_rows, link_ref, table_sem.at[3]),
        pltpu.make_async_copy(scale_row, scale_ref, table_sem.at[4]),
    ]
    for copy in to_scalars:
        copy.start()
    for copy in to_scalars:
        copy.wait()

    sums[0] = jnp.zeros(sums.shape[1:], jnp.float32)

    def add_slot(slot, carry):
        sums[slot + 1] = (
            tiles[slot].astype(jnp.float32) * scale_ref[0, slot] + sums[link_ref[0, slot]]
        )
        return carry

    for index in range(LOAD_PARTS):
        load(index).wait()
        lax.fori_loop(index * part, (index + 1) * part, add_slot, 0)

    for step in range(1, min(au.half, 2)):
        gather_item.forward(step)

    def place_row(row, carry):
        for column in range(item_tiles):
            place = row * item_tiles + column
            tile = sums[link_ref[1 + place // cap, place % cap]]
            adjacency[
                pl.ds(pl.multiple_of(row * edge, edge), edge), pl.ds(column * edge, edge)
            ] = tile.astype(jnp.bfloat16)
        return carry

    lax.fori_loop(0, user_tiles, place_row, 0)

    for step in range(2, au.half):
        gather_item.forward(step)
    for step in range(1, ia.half):
        gather_user.forward(step)

    wide = 2 * edge
    for copy in own_loads:
        copy.wait()
    gather_user.finish()

    def item_product(index, carry):
        start = pl.multiple_of(index * wide, wide)
        product = dot(adjacency[:, pl.ds(start, wide)], user_full[...], ((0,), (0,)))
        item_terms[pl.ds(start, wide), :] = product.astype(jnp.bfloat16)
        return carry

    lax.fori_loop(0, items // wide, item_product, 0)
    reduce_item = Reduce(
        au, item_terms, item_near, item_out, item_far, [au_reduce_sems.at[i] for i in range(4)]
    )
    reduce_item.start()

    gather_item.finish()

    def user_product(index, carry):
        start = pl.multiple_of(index * wide, wide)
        product = dot(adjacency[pl.ds(start, wide), :], item_full[...], ((1,), (0,)))
        user_terms[pl.ds(start, wide), :] = product.astype(jnp.bfloat16)
        return carry

    lax.fori_loop(0, users // wide, user_product, 0)
    reduce_user = Reduce(
        ia, user_terms, user_near, user_out, user_far, [ia_reduce_sems.at[i] for i in range(4)]
    )
    reduce_user.start()
    reduce_user.pass_on()
    reduce_item.pass_on()

    q_user = reduce_user.finish()
    user_low = q_user.astype(jnp.bfloat16)
    out_user[...] = dot(user_low, weight[...], ((1,), (1,))).astype(jnp.bfloat16)
    keep_user = pltpu.make_async_copy(out_user, out_user_hbm, own_sem.at[5])
    keep_item = pltpu.make_async_copy(out_item, out_item_hbm, own_sem.at[6])
    keep_user.start()
    term = embedded_product(user_emb[...], q_user, user_low)
    q_item = reduce_item.finish()
    item_low = q_item.astype(jnp.bfloat16)
    term = term + embedded_product(item_emb[...], q_item, item_low)

    if in_kernel:
        piece_rows = piece_out.shape[1]
        columns = out_weight.shape[1] // LANES
        for index in range(count):
            row, column = index // columns, index % columns
            piece_out[index] = term[
                row * piece_rows : (row + 1) * piece_rows, column * LANES : (column + 1) * LANES
            ].astype(jnp.bfloat16)

        def scatter(step):
            target = (me + step) % count
            return remote(
                piece_out.at[target],
                piece_land.at[step],
                piece_sems.at[0, step],
                piece_sems.at[1, step],
                peer(target),
            )

        def spread(step, arriving=False):
            origin = (me + count - step) % count
            return remote(
                piece_own,
                piece_all.at[origin if arriving else me],
                piece_sems.at[2, step],
                piece_sems.at[3, step],
                peer((me + step) % count),
            )

        def run(action):
            for step in range(1, count):
                action(step)

        run(lambda step: scatter(step).start())
        out_item[...] = dot(item_low, weight[...], ((1,), (1,))).astype(jnp.bfloat16)
        keep_item.start()
        run(lambda step: scatter(step).wait_recv())
        total = piece_out[me].astype(jnp.float32)
        for step in range(1, count):
            total = total + piece_land[step].astype(jnp.float32)
        piece_own[...] = total.astype(jnp.bfloat16)
        run(lambda step: spread(step).start())
        piece_all[me] = piece_own[...]
        run(lambda step: spread(step, True).wait_recv())
        for index in range(count):
            row, column = index // columns, index % columns
            out_weight[
                row * piece_rows : (row + 1) * piece_rows, column * LANES : (column + 1) * LANES
            ] = (piece_all[index].astype(jnp.float32) * factor)
        run(lambda step: scatter(step).wait_send())
        run(lambda step: spread(step).wait_send())
    else:
        out_item[...] = dot(item_low, weight[...], ((1,), (1,))).astype(jnp.bfloat16)
        keep_item.start()
        out_weight[...] = term * factor

    keep_user.wait()
    keep_item.wait()
    gather_user.drain()
    gather_item.drain()
    reduce_user.drain()
    reduce_item.drain()


def hand_on(*refs):
    sems = refs[-1]
    half = (len(refs) - 1) // 2
    copies = [
        pltpu.make_async_copy(refs[index], refs[half + index], sems.at[index])
        for index in range(half)
    ]
    for copy in copies:
        copy.start()
    for copy in copies:
        copy.wait()


def per_device(
    user_emb,
    item_emb,
    weight,
    grad_user,
    grad_item,
    tile_values,
    tile_rows,
    tile_cols,
    tile_norm,
    tile_count,
):
    n_au, n_ia = lax.axis_size("au"), lax.axis_size("ia")
    count = n_au * n_ia
    width = weight.shape[0]
    cap, edge = tile_values.shape[1:3]
    user_rows, item_rows = user_emb.shape[1], item_emb.shape[1]
    users, items = user_rows * n_ia, item_rows * n_au
    item_tiles = items // edge
    places = (users // edge) * item_tiles

    link_rows = 1 + -(-places // cap)
    piece_rows = width * (width // LANES) // count
    in_kernel = piece_rows % 16 == 0 and piece_rows > 0 and width % piece_rows == 0
    pieces = count if in_kernel else 1
    piece_rows = piece_rows if in_kernel else 16
    factor = 1.0 / math.sqrt(users * n_au + items * n_ia)
    half_au, half_ia = n_au // 2, n_ia // 2
    bf16, f32 = jnp.bfloat16, jnp.float32
    vmem = pl.BlockSpec(memory_space=pltpu.VMEM)
    hbm = pl.BlockSpec(memory_space=pltpu.HBM)
    smem = pl.BlockSpec(memory_space=pltpu.SMEM)
    dma = pltpu.SemaphoreType.DMA

    outs = pl.pallas_call(
        functools.partial(kernel, (n_au, n_ia, in_kernel, factor)),
        out_shape=(
            jax.ShapeDtypeStruct((user_rows, width), bf16),
            jax.ShapeDtypeStruct((item_rows, width), bf16),
            jax.ShapeDtypeStruct((width, width), f32),
        ),
        in_specs=[smem] + [hbm] * 9,
        out_specs=(hbm, hbm, vmem),
        scratch_shapes=[
            pltpu.VMEM((user_rows, width), bf16),
            pltpu.VMEM((item_rows, width), bf16),
            pltpu.VMEM((user_rows, width), bf16),
            pltpu.VMEM((item_rows, width), bf16),
            pltpu.VMEM((width, width), bf16),
            pltpu.VMEM((3, 1, cap), jnp.int32),
            pltpu.VMEM((link_rows, cap), jnp.int32),
            pltpu.VMEM((1, cap), f32),
            pltpu.SMEM((link_rows, cap), jnp.int32),
            pltpu.SMEM((1, cap), f32),
            pltpu.VMEM((cap, edge, edge), bf16),
            pltpu.VMEM((cap + 1, edge, edge), f32),
            pltpu.VMEM((users, items), bf16),
            pltpu.VMEM((users, width), bf16),
            pltpu.VMEM((items, width), bf16),
            pltpu.VMEM((users, width), bf16),
            pltpu.VMEM((items, width), bf16),
            pltpu.VMEM((half_ia, user_rows, width), bf16),
            pltpu.VMEM((half_ia, user_rows, width), bf16),
            pltpu.VMEM((half_ia, user_rows, width), bf16),
            pltpu.VMEM((half_au, item_rows, width), bf16),
            pltpu.VMEM((half_au, item_rows, width), bf16),
            pltpu.VMEM((half_au, item_rows, width), bf16),
            pltpu.VMEM((pieces, piece_rows, LANES), bf16),
            pltpu.VMEM((pieces, piece_rows, LANES), bf16),
            pltpu.VMEM((piece_rows, LANES), bf16),
            pltpu.VMEM((pieces, piece_rows, LANES), bf16),
            dma((LOAD_PARTS,)),
            dma((7,)),
            dma((5,)),
            dma((4, half_ia)),
            dma((4, half_au)),
            dma((4, half_ia)),
            dma((4, half_au)),
            dma((4, pieces)),
        ],
        compiler_params=pltpu.CompilerParams(
            collective_id=0, has_side_effects=True, vmem_limit_bytes=62 * 1024 * 1024
        ),
    )(
        tile_count,
        tile_rows,
        tile_cols,
        tile_norm,
        user_emb[0],
        item_emb[0],
        weight,
        grad_user[0],
        grad_item[0],
        tile_values[0],
    )
    grad_user_emb, grad_item_emb, grad_weight = pl.pallas_call(
        hand_on,
        out_shape=tuple(jax.ShapeDtypeStruct(out.shape, out.dtype) for out in outs),
        in_specs=[hbm] * len(outs),
        out_specs=(hbm,) * len(outs),
        scratch_shapes=[dma((len(outs),))],
        compiler_params=pltpu.CompilerParams(vmem_limit_bytes=62 * 1024 * 1024),
    )(*outs)
    if not in_kernel:
        grad_weight = lax.psum(grad_weight, ("au", "ia"))
    return (grad_user_emb[None], grad_item_emb[None], grad_weight)


def solution(mesh):
    return jax.shard_map(
        per_device,
        mesh=mesh,
        in_specs=(
            P("au", "ia", None),
            P("ia", "au", None),
            P(),
            P("au", "ia", None),
            P("ia", "au", None),
            P("au", "ia", None, None),
            P("au", "ia"),
            P("au", "ia"),
            P("au", "ia"),
            P("au", "ia"),
        ),
        out_specs=(P("au", "ia", None), P("ia", "au", None), P()),
        check_vma=False,
    )
```
